256 devices in a mesh: row: 8 (over z), col: 16 (over y, x), layer: 2 (over core).
Axes of the slice: x: 4, y: 4, z: 8, core: 2. Of those that a mesh axis runs over, the one named last changes fastest.
Arguments:
- density: bfloat16 [8192, 8192], P('row', ('col', 'layer')), may hold values from -3 to 3
- block_mask: int32 [64, 64], P('row', ('col', 'layer')), may hold values from 0 to 1, as said below
- keep_mask: int32 [64, 64], P('row', ('col', 'layer')), may hold values 0 or 1
- branch_flag: int32 [64], P('row'), may hold values from 0 to 1
Outputs:
- updated: float32 [8192, 8192], P('row', ('col', 'layer'))
- trace_new: float32 [], replicated
The draws below stay inside these ranges and needn't reach their ends.
Inputs may be any that keep to these rules, and one draw needn't show every extreme that they name: `block_mask`: symmetric, 1 on the diagonal; 1 where two blocks' centres in a periodic box lie within a cutoff distance of each other, else 0; block labels are in no spatial order. `keep_mask`: 0 or 1 for each block.
All inputs are finite; a program needn't handle non-finite values.
Results may differ from the reference program's by a relative error of at most 0.0004.
Values may be sent and summed in bfloat16 or wider, within the bound.
No kernel may reach another device: no remote copies, remote signals or barrier semaphores. Data moves between devices by JAX's collectives and lax.ppermute only.
A program may use at most 64 MiB of HBM per device.

```python
import jax
import jax.numpy as jnp
from jax import lax

BLK = 128
NB = 64
N = 8192


def morton_coord(indices, offset):
    coord = jnp.zeros_like(indices)
    for level in range(11):
        digit = indices >> 3 * level + offset & 1
        coord = coord + (digit << level)
    return coord


def draw_block_mask(key, part):
    indices = jnp.arange(NB, dtype=jnp.int32)
    jitter = jax.random.randint(jax.random.fold_in(key, 7), (3, NB), 0, 4, dtype=jnp.int32)
    squared = jnp.zeros((NB, NB), jnp.int32)
    for offset in range(3):
        grid = morton_coord(indices, offset)
        extent = 4 * (jnp.max(grid) + 1)
        place = 4 * grid + jitter[offset]
        apart = jnp.abs(place[:, None] - place[None, :]) % extent
        apart = jnp.minimum(apart, extent - apart)
        squared = squared + apart * apart
    cutoff = int((3.8 * NB) ** (2.0 / 3.0))
    base = (squared <= cutoff).astype(jnp.int32)
    order = jax.random.permutation(jax.random.fold_in(key, 11), NB).astype(jnp.int32)
    return base[order][:, order]


def touch_ends(entries, stream_key, low, largest):
    shape = entries.shape
    spot = [jax.random.randint(jax.random.fold_in(stream_key, axis), (), 0, shape[axis]) for axis in range(len(shape))]
    entries = entries.at[tuple(spot)].set(low)
    longest = shape.index(max(shape))
    spot[longest] = (spot[longest] + 1) % shape[longest]
    return entries.at[tuple(spot)].set(largest)


def steps_of(stream_key, dims, shards, least, top_value):
    loudness, own = 1.0, jax.random.fold_in(stream_key, 6)
    for axis_at, parts in shards:
        draws = jnp.exp(jax.random.uniform(jax.random.fold_in(own, axis_at), (parts,), jnp.float32, least / len(shards), top_value / len(shards)))
        loudness = loudness * jnp.repeat(draws, dims[axis_at] // parts).reshape([-1 if axis == axis_at else 1 for axis in range(len(dims))])
    return loudness


def gaussian(stream_key, shape, scale, bound, pieces=(), kind=jnp.bfloat16):
    factor_of = steps_of(stream_key, shape, pieces, -0.22, 0.18) if pieces else 1.0
    drawn = jax.random.normal(stream_key, shape, jnp.float32) * scale * factor_of
    return jnp.minimum(jnp.maximum(drawn, -bound), bound).astype(kind)


def setup_inputs(seed: int = 0) -> dict:
    arg_keys = jax.random.split(jax.random.key(seed), 5)
    return {
        "density": gaussian(arg_keys[0], (N, N), ((N // 16) ** -0.25), 3.0, ((0, 8), (1, 32))),
        "block_mask": draw_block_mask(jax.random.fold_in(arg_keys[4], 71), 0),
        "keep_mask": touch_ends((jax.random.randint(arg_keys[2], (NB, NB), 0, 2) < 1).astype(jnp.int32), jax.random.fold_in(arg_keys[2], 1), 0, 1),
        "branch_flag": touch_ends(jax.random.randint(arg_keys[3], (NB,), 0, 2), jax.random.fold_in(arg_keys[3], 1), 0, 1).astype(jnp.int32),
    }


def expand_mask(block_mask):
    return jnp.repeat(jnp.repeat(block_mask, BLK, axis=0), BLK, axis=1)


def reference(density, block_mask, keep_mask, branch_flag):
    masked = density * expand_mask(block_mask).astype(jnp.bfloat16)
    wide = masked.astype(jnp.float32)
    square = jnp.dot(wide, wide, precision=lax.Precision.HIGHEST, preferred_element_type=jnp.float32)
    doubled = 2.0 * wide - square
    flag_rows = jnp.repeat(branch_flag, BLK)[:, None]
    chosen = jnp.where(flag_rows == 1, square, doubled)
    updated = chosen * expand_mask(keep_mask).astype(jnp.float32)
    trace_new = jnp.trace(updated)
    return updated, trace_new
```

```python
import functools

import jax
import jax.numpy as jnp
from jax import lax
from jax.experimental import pallas as pl
from jax.experimental.pallas import tpu as pltpu
from jax.sharding import Mesh
from jax.sharding import PartitionSpec as P

BLK = 128
Y, X = "col_0", "col_1"
COL_LAYER = (Y, X, "layer")
SMEM = pl.BlockSpec(memory_space=pltpu.SMEM)
VMEM = pl.BlockSpec(memory_space=pltpu.VMEM)
HBM = pl.BlockSpec(memory_space=pl.ANY)
PARAMS = pltpu.CompilerParams(vmem_limit_bytes=48 * 1024 * 1024)
ORDER4 = (0, -1, 1, 2)


def shift(value, axis, off):
    n = lax.axis_size(axis)
    return lax.ppermute(value, axis, [(i, (i + off) % n) for i in range(n)])


def ring4(own, axis):
    half = own.shape[0] // 2
    plus, minus = shift(own, axis, 1), shift(own, axis, -1)
    return plus, minus, shift(plus[:half], axis, 1), shift(minus[half:], axis, -1)


def ring8(own, axis):
    half = own.shape[0] // 2
    plus, minus = [own], [own]
    for _ in range(3):
        plus.append(shift(plus[-1], axis, 1))
        minus.append(shift(minus[-1], axis, -1))
    far = (shift(plus[-1][:half], axis, 1), shift(minus[-1][half:], axis, -1))
    return plus[1:], minus[1:], far


def mask_kernel(pos, bm, x, m, top, low, own, peer):
    layer = pos[3]
    rows = []
    for i in range(8):
        parts = [
            x[pl.ds(i * BLK, BLK), pl.ds(j * BLK, BLK)] * bm[i, j].astype(jnp.float32).astype(jnp.bfloat16)
            for j in range(2)
        ]
        rows.append(jnp.concatenate(parts, axis=1))
    for i in range(8):
        m[pl.ds(i * BLK, BLK), :] = rows[i]
        half = top if i < 4 else low
        half[pl.ds((i % 4) * BLK, BLK), :] = rows[i]
        at, cls, inner = i // 4, (i // 2) % 2, i % 2

        @pl.when(layer == cls)
        def _():
            own[at, pl.ds(inner * BLK, BLK), :] = rows[i]

        @pl.when(layer != cls)
        def _():
            peer[at, pl.ds(inner * BLK, BLK), :] = rows[i]


def place(pos, d, half):
    r, y, x = pos[0], pos[1], pos[2]
    src = lax.rem(r - d + 8, 8)
    col = src * 2 + half
    dy, dx = lax.rem(col // 4 - y + 4, 4), lax.rem(lax.rem(col, 4) - x + 4, 4)
    rank = lambda o: jnp.where(o == 0, 0, jnp.where(o == 3, 1, jnp.where(o == 1, 2, 3)))
    return rank(dy), rank(dx)


def load_b(pos, z_refs, by, bx, sems):
    copies = []
    pieces = [(d, ch, rh, z_refs[d].at[2 * ch + rh]) for d in range(4) for ch in range(2) for rh in range(2)]
    pieces += [(-d, ch, rh, z_refs[3 + d].at[2 * ch + rh]) for d in range(1, 4) for ch in range(2) for rh in range(2)]
    pieces += [(4, ch, rh, z_refs[7 + ch].at[rh]) for ch in range(2) for rh in range(2)]
    for d, ch, rh, src in pieces:
        ry, rx = place(pos, d, rh)
        cols = pl.ds(ch * 256, 256)
        for dst, at in ((by, ry * 4 + rx), (bx, rx * 4 + ry)):
            copies.append(pltpu.make_async_copy(src, dst.at[pl.ds(pl.multiple_of(at * 256, 256), 256), cols], sems.at[len(copies)]))
    return copies


def near_kernel(pos, *refs):
    z_refs, (t0, t1, t2, l0, l1, l2) = refs[:9], refs[9:15]
    p_own, p_peer, by_out, bx_out = refs[15:19]
    by, bx, a_top, a_low, sem_b, sem_a, sem_o = refs[19:]
    copies = load_b(pos, z_refs, by, bx, sem_b)
    n = 0
    for dst, srcs in ((a_top, (t0, t1, t2)), (a_low, (l0, l1, l2))):
        for g, src in enumerate(srcs):
            for k in range(4):
                copies.append(
                    pltpu.make_async_copy(src.at[pl.ds(k * 512, 512), :], dst.at[:, pl.ds((4 * g + k) * 256, 256)], sem_a.at[n])
                )
                n += 1
    for c in copies:
        c.start()
    for c in copies:
        c.wait()
    outs = [
        pltpu.make_async_copy(by.at[pl.ds(3072, 1024), :], by_out, sem_o.at[0]),
        pltpu.make_async_copy(bx.at[pl.ds(3072, 1024), :], bx_out, sem_o.at[1]),
    ]
    for c in outs:
        c.start()
    for base, a, b in ((0, a_top, by), (512, a_low, bx)):

        @pl.loop(0, 2)
        def _(i):
            rows = pl.ds(pl.multiple_of(i * 256, 256), 256)
            to = pl.ds(pl.multiple_of(base + i * 256, 256), 256)
            out = jnp.dot(a[rows, :], b[pl.ds(0, 3072), :], preferred_element_type=jnp.float32)
            p_own[to, :] = out[:, :256]
            p_peer[to, :] = out[:, 256:]

    for c in outs:
        c.wait()


def far_kernel(by, bx, q_top0, q_top1, q_low0, q_low1, p_own, p_peer, o_own, o_peer):
    for base, qs, b in ((0, (q_top0, q_top1), by), (512, (q_low0, q_low1), bx)):
        for i in range(2):
            to = pl.ds(base + i * 256, 256)
            a = jnp.concatenate(
                [qs[k // 2][pl.ds((k % 2) * 512 + i * 256, 256), :] for k in range(4)], axis=1
            )
            out = jnp.dot(a, b[...], preferred_element_type=jnp.float32)
            o_peer[to, :] = p_peer[to, :] + out[:, 256:]
            o_own[to, :] = p_own[to, :] + out[:, :256]


def final_kernel(pos, keep, flag, own, recv, m, out, trace):
    first = (pos[1] * 8 + pos[2] * 2 + pos[3]) * 2 - pos[0] * 8
    total = jnp.zeros((BLK, BLK), jnp.float32)
    eye = lax.broadcasted_iota(jnp.int32, (BLK, BLK), 0) == lax.broadcasted_iota(jnp.int32, (BLK, BLK), 1)
    for i in range(8):
        take = flag[i] == 1
        sign, twice = jnp.where(take, 1.0, -1.0), jnp.where(take, 0.0, 2.0)
        for j in range(2):
            at = (pl.ds(i * BLK, BLK), pl.ds(j * BLK, BLK))
            square = own[at] + recv[at]
            value = (twice * m[at].astype(jnp.float32) + sign * square) * keep[i, j].astype(jnp.float32)
            out[at] = value
            here = (first + j == i).astype(jnp.float32)
            total = total + jnp.where(eye, value, 0.0) * here
    trace[...] = jnp.sum(total.reshape(16, 8, BLK), axis=0)


def bf16(*shape):
    return jax.ShapeDtypeStruct(shape, jnp.bfloat16)


def f32(*shape):
    return jax.ShapeDtypeStruct(shape, jnp.float32)


def sum_all(value):
    for axes, n in (((Y, X), 16), ("row", 8)):
        spread = jnp.broadcast_to(value[None], (n, 8, BLK))
        value = jnp.sum(lax.all_to_all(spread, axes, 0, 0), axis=0)
    return jnp.sum(value + lax.ppermute(value, "layer", [(0, 1), (1, 0)]))


def on_device(density, block_mask, keep_mask, branch_flag):
    pos = jnp.stack([lax.axis_index(a) for a in ("row", Y, X, "layer")]).astype(jnp.int32)
    swap = [(0, 1), (1, 0)]
    m, top, low, own_rows, peer_rows = pl.pallas_call(
        mask_kernel,
        out_shape=[bf16(1024, 256), bf16(512, 256), bf16(512, 256), bf16(2, 256, 256), bf16(2, 256, 256)],
        in_specs=[SMEM, SMEM, VMEM],
        out_specs=[VMEM] * 5,
        compiler_params=PARAMS,
        name="mask",
    )(pos, block_mask, density)
    other = lax.ppermute(peer_rows, "layer", swap)
    z_tile = jnp.concatenate([own_rows, other], axis=0)
    z_plus, z_minus, z_far = ring8(z_tile, "row")
    row_top = jnp.concatenate([top, *ring4(top, X)], axis=0)
    row_low = jnp.concatenate([low, *ring4(low, Y)], axis=0)
    top_p, top_m, top_q0, top_q1 = ring4(row_top, Y)
    low_p, low_m, low_q0, low_q1 = ring4(row_low, X)
    p_own, p_peer, by, bx = pl.pallas_call(
        near_kernel,
        out_shape=[f32(1024, 256), f32(1024, 256), bf16(1024, 512), bf16(1024, 512)],
        in_specs=[SMEM] + [HBM] * 15,
        out_specs=[VMEM, VMEM, HBM, HBM],
        scratch_shapes=[
            pltpu.VMEM((4096, 512), jnp.bfloat16),
            pltpu.VMEM((4096, 512), jnp.bfloat16),
            pltpu.VMEM((512, 3072), jnp.bfloat16),
            pltpu.VMEM((512, 3072), jnp.bfloat16),
            pltpu.SemaphoreType.DMA((64,)),
            pltpu.SemaphoreType.DMA((24,)),
            pltpu.SemaphoreType.DMA((2,)),
        ],
        compiler_params=PARAMS,
        name="near",
        cost_estimate=pl.CostEstimate(flops=3_200_000_000, bytes_accessed=12_000_000, transcendentals=0),
    )(pos, z_tile, *z_plus, *z_minus, *z_far, row_top, top_p, top_m, row_low, low_p, low_m)
    p_own, p_peer = pl.pallas_call(
        far_kernel,
        out_shape=[f32(1024, 256), f32(1024, 256)],
        in_specs=[VMEM] * 8,
        out_specs=[VMEM, VMEM],
        input_output_aliases={6: 0, 7: 1},
        compiler_params=PARAMS,
        name="far",
        cost_estimate=pl.CostEstimate(flops=1_100_000_000, bytes_accessed=4_000_000, transcendentals=0),
    )(by, bx, top_q0, top_q1, low_q0, low_q1, p_own, p_peer)
    recv = lax.ppermute(p_peer, "layer", swap)
    updated, local_trace = pl.pallas_call(
        final_kernel,
        out_shape=[f32(1024, 256), f32(8, BLK)],
        in_specs=[SMEM, SMEM, SMEM, VMEM, VMEM, VMEM],
        out_specs=[VMEM, VMEM],
        compiler_params=PARAMS,
        name="final",
    )(pos, keep_mask, branch_flag, p_own, recv, m)
    return (updated, sum_all(local_trace))


def solution(mesh):
    split = Mesh(
        mesh.devices.reshape(mesh.shape["row"], 4, 4, mesh.shape["layer"]),
        ("row", Y, X, "layer"),
    )
    in_specs = (P("row", COL_LAYER), P("row", COL_LAYER), P("row", COL_LAYER), P("row"))
    out_specs = (P("row", COL_LAYER), P())
    return jax.shard_map(
        on_device, mesh=split, in_specs=in_specs, out_specs=out_specs, check_vma=False
    )
```

```python
import functools

import jax
import jax.numpy as jnp
from jax import lax
from jax.experimental import pallas as pl
from jax.experimental.pallas import tpu as pltpu
from jax.sharding import Mesh
from jax.sharding import PartitionSpec as P

BLK = 128
Y, X = "col_0", "col_1"
COL_LAYER = (Y, X, "layer")
SMEM = pl.BlockSpec(memory_space=pltpu.SMEM)
VMEM = pl.BlockSpec(memory_space=pltpu.VMEM)
HBM = pl.BlockSpec(memory_space=pl.ANY)


def room(mib):
    return pltpu.CompilerParams(vmem_limit_bytes=mib * 1024 * 1024)


def shift(value, axis, off):
    n = lax.axis_size(axis)
    return lax.ppermute(value, axis, [(i, (i + off) % n) for i in range(n)])


def turn(value, stage, off):
    nz, ny, nx = (lax.axis_size(a) for a in ("row", Y, X))
    at = lambda z, y, x, core: ((z * ny + y) * nx + x) * 2 + core
    pairs = []
    for z in range(nz):
        for y in range(ny):
            for x in range(nx):
                for core in range(2):
                    along_x = core == stage
                    to = (y, (x + off) % nx) if along_x else ((y + off) % ny, x)
                    pairs.append((at(z, y, x, core), at(z, *to, core)))
    return lax.ppermute(value, ("row", Y, X, "layer"), pairs)


def keep_kernel(x, out):
    pass


def hold(value, us):
    return pl.pallas_call(
        keep_kernel,
        out_shape=jax.ShapeDtypeStruct(value.shape, value.dtype),
        in_specs=[HBM],
        out_specs=HBM,
        input_output_aliases={0: 0},
        compiler_params=room(1),
        name="hold",
        cost_estimate=pl.CostEstimate(flops=int(us * 1e9), bytes_accessed=0, transcendentals=0),
    )(value)


def ring4(own, stage):
    half = own.shape[0] // 2
    plus, minus = turn(own, stage, 1), turn(own, stage, -1)
    return plus, minus, turn(plus[:half], stage, 1), turn(minus[half:], stage, -1)


def ring8(own, axis):
    half = own.shape[0] // 2
    plus, minus = [own], [own]
    for _ in range(3):
        plus.append(hold(shift(plus[-1], axis, 1), 4.0))
        minus.append(hold(shift(minus[-1], axis, -1), 4.0))
    far = (shift(plus[-1][:half], axis, 1), shift(minus[-1][half:], axis, -1))
    return plus[1:], minus[1:], far


def mask_kernel(pos, bm, x, m, own, peer):
    layer = pos[3]
    rows = []
    for i in range(8):
        parts = [
            x[pl.ds(i * BLK, BLK), pl.ds(j * BLK, BLK)] * bm[j, i].astype(jnp.float32).astype(jnp.bfloat16)
            for j in range(2)
        ]
        rows.append(jnp.concatenate(parts, axis=1))
    for i in range(8):
        m[pl.ds(i * BLK, BLK), :] = rows[i]
        at, cls, inner = i // 4, (i // 2) % 2, i % 2

        @pl.when(layer == cls)
        def _():
            own[at, pl.ds(inner * BLK, BLK), :] = rows[i]

        @pl.when(layer != cls)
        def _():
            peer[at, pl.ds(inner * BLK, BLK), :] = rows[i]


def place(pos, d, half):
    r, y, x = pos[0], pos[1], pos[2]
    src = lax.rem(r - d + 8, 8)
    col = src * 2 + half
    dy, dx = lax.rem(col // 4 - y + 4, 4), lax.rem(lax.rem(col, 4) - x + 4, 4)
    rank = lambda o: jnp.where(o == 0, 0, jnp.where(o == 3, 1, jnp.where(o == 1, 2, 3)))
    return rank(dy), rank(dx)


def rows_kernel(pos, *refs):
    z_refs, b = refs[:9], refs[9]
    pieces = [(d, ch, rh, d, 2 * ch + rh) for d in range(4) for ch in range(2) for rh in range(2)]
    pieces += [(-d, ch, rh, 3 + d, 2 * ch + rh) for d in range(1, 4) for ch in range(2) for rh in range(2)]
    pieces += [(4, ch, rh, 7 + ch, rh) for ch in range(2) for rh in range(2)]
    for d, ch, rh, ref, at in pieces:
        ry, rx = place(pos, d, rh)
        to = jnp.where(pos[3] == 0, ry * 4 + rx, rx * 4 + ry)
        b[ch, pl.ds(pl.multiple_of(to * 256, 256), 256), :] = z_refs[ref][at]


def near_kernel(b, line, line_p, line_m, p_own, p_peer):
    @pl.loop(0, 4)
    def _(i):
        a = []
        for src in (line, line_p, line_m):
            for k in range(4):
                a.append(src[pl.ds(pl.multiple_of(k * 1024 + i * 256, 256), 256), :])
        rows = pl.ds(pl.multiple_of(i * 256, 256), 256)
        a = jnp.concatenate(a, axis=1)
        p_peer[rows, :] = jnp.dot(a, b[1, pl.ds(0, 3072), :], preferred_element_type=jnp.float32)
        p_own[rows, :] = jnp.dot(a, b[0, pl.ds(0, 3072), :], preferred_element_type=jnp.float32)


def far_rows(b, q0, q1, ch, old, new):
    for i in range(4):
        rows = pl.ds(i * 256, 256)
        a = jnp.concatenate([(q0, q1)[k // 2][pl.ds((k % 2) * 1024 + i * 256, 256), :] for k in range(4)], axis=1)
        new[rows, :] = old[rows, :] + jnp.dot(a, b[ch, pl.ds(3072, 1024), :], preferred_element_type=jnp.float32)


def far_own_kernel(b, q0, q1, p_own, tie, new):
    far_rows(b, q0, q1, 0, p_own, new)


def far_peer_kernel(pos, keep, flag, m, b, q0, q1, p_own, p_peer, new, out):
    lane = lax.broadcasted_iota(jnp.int32, (1, BLK), 1)
    eye = lax.broadcasted_iota(jnp.int32, (BLK, BLK), 0) == lax.broadcasted_iota(jnp.int32, (BLK, BLK), 1)
    chip, core = pos[1] * 4 + pos[2], pos[3]
    out[...] = jnp.zeros((1, BLK), jnp.float32)
    far_rows(b, q0, q1, 1, p_peer, new)

    def trace(block):
        line = jnp.sum(jnp.where(eye, block, 0.0), axis=0, keepdims=True)
        return jnp.sum(line, axis=1, keepdims=True)

    @pl.when(chip // 2 == pos[0])
    def _():
        total = jnp.zeros((1, BLK), jnp.float32)
        for ch in range(2):
            side = core if ch == 0 else 1 - core
            for j in range(2):
                i = (chip % 2) * 4 + side * 2 + j
                start = pl.multiple_of(i * BLK, BLK)
                rows, cols = pl.ds(start, BLK), pl.ds(j * BLK, BLK)
                if ch == 1:
                    block = new[rows, cols]
                else:
                    block = p_own[rows, cols]
                    for k in range(4):
                        a = (q0, q1)[k // 2][pl.ds(pl.multiple_of((k % 2) * 1024 + start, BLK), BLK), :]
                        block += jnp.dot(a, b[ch, pl.ds(3072 + k * 256, 256), cols], preferred_element_type=jnp.float32)
                total += jnp.where(lane == i, trace(block), 0.0)
                if ch == 0:
                    total += jnp.where(lane == 8 + i, keep[j, i].astype(jnp.float32), 0.0)
                    total += jnp.where(lane == 16 + i, trace(m[rows, cols].astype(jnp.float32)), 0.0)
                    total += jnp.where(lane == 24 + i, flag[i].astype(jnp.float32), 0.0)
        out[...] = total


def final_kernel(keep, flag, own, recv, m, out):
    for i in range(8):
        take = flag[i] == 1
        sign, twice = jnp.where(take, 1.0, -1.0), jnp.where(take, 0.0, 2.0)
        for j in range(2):
            at = (pl.ds(i * BLK, BLK), pl.ds(j * BLK, BLK))
            square = own[at] + recv[at]
            out[at] = (twice * m[at].astype(jnp.float32) + sign * square) * keep[j, i].astype(jnp.float32)


def bf16(*shape):
    return jax.ShapeDtypeStruct(shape, jnp.bfloat16)


def f32(*shape):
    return jax.ShapeDtypeStruct(shape, jnp.float32)


def trace_of(parts):
    spread = jnp.broadcast_to(parts[None], (128, 1, BLK))
    rows = lax.all_to_all(spread, ("row", Y, X), 0, 0).reshape(8, 16, BLK).sum(axis=1)
    rows = rows + lax.ppermute(rows, "layer", [(0, 1), (1, 0)])
    square, keep, linear, branch = (rows[:, 8 * n : 8 * n + 8] for n in range(4))
    return jnp.sum(keep * jnp.where(branch == 1.0, square, 2.0 * linear - square))


def on_device(density, block_mask, keep_mask, branch_flag):
    pos = jnp.stack([lax.axis_index(a) for a in ("row", Y, X, "layer")]).astype(jnp.int32)
    swap = [(0, 1), (1, 0)]
    m, own_rows, peer_rows = pl.pallas_call(
        mask_kernel,
        out_shape=[bf16(1024, 256), bf16(2, 256, 256), bf16(2, 256, 256)],
        in_specs=[SMEM, SMEM, VMEM],
        out_specs=[VMEM] * 3,
        compiler_params=room(6),
        name="mask",
    )(pos, block_mask.T, density)
    other = lax.ppermute(peer_rows, "layer", swap)
    z_tile = jnp.concatenate([own_rows, other], axis=0)
    z_plus, z_minus, z_far = ring8(z_tile, "row")
    line = jnp.concatenate([m, *ring4(m, 0)], axis=0)
    line_p, line_m, q0, q1 = ring4(line, 1)
    inner = pl.pallas_call(
        rows_kernel,
        out_shape=bf16(2, 4096, 256),
        in_specs=[SMEM] + [VMEM] * 9,
        out_specs=VMEM,
        compiler_params=room(10),
        name="rows",
        cost_estimate=pl.CostEstimate(flops=30_000_000_000, bytes_accessed=8_000_000, transcendentals=0),
    )(pos, z_tile, *z_plus, *z_minus, *z_far)
    p_own, p_peer = pl.pallas_call(
        near_kernel,
        out_shape=[f32(1024, 256), f32(1024, 256)],
        in_specs=[VMEM] * 4,
        out_specs=[VMEM, VMEM],
        compiler_params=room(14),
        name="near",
        cost_estimate=pl.CostEstimate(flops=3_200_000_000, bytes_accessed=12_000_000, transcendentals=0),
    )(inner, line, line_p, line_m)
    keep = keep_mask.T
    peer_part, parts = pl.pallas_call(
        far_peer_kernel,
        out_shape=[f32(1024, 256), f32(1, BLK)],
        in_specs=[SMEM, SMEM, SMEM] + [VMEM] * 6,
        out_specs=[VMEM, VMEM],
        compiler_params=room(14),
        name="far_peer",
        cost_estimate=pl.CostEstimate(flops=540_000_000, bytes_accessed=4_000_000, transcendentals=0),
    )(pos, keep, branch_flag, m, inner, q0, q1, p_own, p_peer)
    own_part = pl.pallas_call(
        far_own_kernel,
        out_shape=f32(1024, 256),
        in_specs=[VMEM] * 5,
        out_specs=VMEM,
        compiler_params=room(10),
        name="far_own",
        cost_estimate=pl.CostEstimate(flops=540_000_000, bytes_accessed=4_000_000, transcendentals=0),
    )(inner, q0, q1, p_own, parts)
    recv = lax.ppermute(peer_part, "layer", swap)
    updated = pl.pallas_call(
        final_kernel,
        out_shape=f32(1024, 256),
        in_specs=[SMEM, SMEM, VMEM, VMEM, VMEM],
        out_specs=VMEM,
        compiler_params=room(6),
        name="final",
        cost_estimate=pl.CostEstimate(flops=2_000_000, bytes_accessed=4_000_000, transcendentals=0),
    )(keep, branch_flag, own_part, recv, m)
    return (updated, trace_of(parts))


def solution(mesh):
    split = Mesh(
        mesh.devices.reshape(mesh.shape["row"], 4, 4, mesh.shape["layer"]),
        ("row", Y, X, "layer"),
    )
    in_specs = (P("row", COL_LAYER), P("row", COL_LAYER), P("row", COL_LAYER), P("row"))
    out_specs = (P("row", COL_LAYER), P())
    return jax.shard_map(
        on_device, mesh=split, in_specs=in_specs, out_specs=out_specs, check_vma=False
    )
```

```python
import functools

import jax
import jax.numpy as jnp
from jax import lax
from jax.experimental import pallas as pl
from jax.experimental.pallas import tpu as pltpu
from jax.sharding import Mesh
from jax.sharding import PartitionSpec as P

BLK = 128
HZ = (6.0, 6.0, 2.0)
HR = 2.0
Y, X = "col_0", "col_1"
COL_LAYER = (Y, X, "layer")
SMEM = pl.BlockSpec(memory_space=pltpu.SMEM)
VMEM = pl.BlockSpec(memory_space=pltpu.VMEM)
HBM = pl.BlockSpec(memory_space=pl.ANY)


def room(mib):
    return pltpu.CompilerParams(vmem_limit_bytes=mib * 1024 * 1024)


def shift(value, axis, off):
    n = lax.axis_size(axis)
    return lax.ppermute(value, axis, [(i, (i + off) % n) for i in range(n)])


def turn(value, stage, off):
    nz, ny, nx = (lax.axis_size(a) for a in ("row", Y, X))
    at = lambda z, y, x, core: ((z * ny + y) * nx + x) * 2 + core
    pairs = []
    for z in range(nz):
        for y in range(ny):
            for x in range(nx):
                for core in range(2):
                    along_x = core == stage
                    to = (y, (x + off) % nx) if along_x else ((y + off) % ny, x)
                    pairs.append((at(z, y, x, core), at(z, *to, core)))
    return lax.ppermute(value, ("row", Y, X, "layer"), pairs)


def keep_kernel(x, out):
    pass


def hold(value, us):
    return pl.pallas_call(
        keep_kernel,
        out_shape=jax.ShapeDtypeStruct(value.shape, value.dtype),
        in_specs=[HBM],
        out_specs=HBM,
        input_output_aliases={0: 0},
        compiler_params=room(1),
        name="hold",
        cost_estimate=pl.CostEstimate(flops=int(us * 1e9), bytes_accessed=0, transcendentals=0),
    )(value)


def ring4(own, stage):
    half = own.shape[0] // 2
    plus, minus = turn(own, stage, 1), turn(own, stage, -1)
    return plus, minus, turn(plus[:half], stage, 1), turn(minus[half:], stage, -1)


def ring8(own, axis):
    plus, minus = [own], [own]
    for cost in HZ:
        plus.append(hold(shift(plus[-1], axis, 1), cost))
        minus.append(hold(shift(minus[-1], axis, -1), cost))
    return plus[1:], minus[1:]


def ring8_end(plus, minus, axis):
    half = plus.shape[0] // 2
    return shift(plus[:half], axis, 1), shift(minus[half:], axis, -1)


def mask_kernel(pos, bm, x, m, own, peer):
    layer = pos[3]
    rows = []
    for i in range(8):
        parts = [
            x[pl.ds(i * BLK, BLK), pl.ds(j * BLK, BLK)] * bm[j, i].astype(jnp.float32).astype(jnp.bfloat16)
            for j in range(2)
        ]
        rows.append(jnp.concatenate(parts, axis=1))
    for i in range(8):
        m[pl.ds(i * BLK, BLK), :] = rows[i]
        at, cls, inner = i // 4, (i // 2) % 2, i % 2

        @pl.when(layer == cls)
        def _():
            own[at, pl.ds(inner * BLK, BLK), :] = rows[i]

        @pl.when(layer != cls)
        def _():
            peer[at, pl.ds(inner * BLK, BLK), :] = rows[i]


def place(pos, d, half):
    r, y, x = pos[0], pos[1], pos[2]
    src = lax.rem(r - d + 8, 8)
    col = src * 2 + half
    dy, dx = lax.rem(col // 4 - y + 4, 4), lax.rem(lax.rem(col, 4) - x + 4, 4)
    rank = lambda o: jnp.where(o == 0, 0, jnp.where(o == 3, 1, jnp.where(o == 1, 2, 3)))
    return rank(dy), rank(dx)


def rows_kernel(pos, *refs):
    z_refs, b = refs[:9], refs[9]
    pieces = [(d, ch, rh, d, 2 * ch + rh) for d in range(4) for ch in range(2) for rh in range(2)]
    pieces += [(-d, ch, rh, 3 + d, 2 * ch + rh) for d in range(1, 4) for ch in range(2) for rh in range(2)]
    pieces += [(4, ch, rh, 7 + ch, rh) for ch in range(2) for rh in range(2)]
    for d, ch, rh, ref, at in pieces:
        ry, rx = place(pos, d, rh)
        to = jnp.where(pos[3] == 0, ry * 4 + rx, rx * 4 + ry)
        b[ch, pl.ds(pl.multiple_of(to * 256, 256), 256), :] = z_refs[ref][at]


def near_kernel(b, line, line_p, line_m, p_own, p_peer):
    @pl.loop(0, 4)
    def _(i):
        a = []
        for src in (line, line_p, line_m):
            for k in range(4):
                a.append(src[pl.ds(pl.multiple_of(k * 1024 + i * 256, 256), 256), :])
        rows = pl.ds(pl.multiple_of(i * 256, 256), 256)
        a = jnp.concatenate(a, axis=1)
        p_peer[rows, :] = jnp.dot(a, b[1, pl.ds(0, 3072), :], preferred_element_type=jnp.float32)
        p_own[rows, :] = jnp.dot(a, b[0, pl.ds(0, 3072), :], preferred_element_type=jnp.float32)


def far_rows(b, q0, q1, ch, old, new):
    for i in range(4):
        rows = pl.ds(i * 256, 256)
        a = jnp.concatenate([(q0, q1)[k // 2][pl.ds((k % 2) * 1024 + i * 256, 256), :] for k in range(4)], axis=1)
        new[rows, :] = old[rows, :] + jnp.dot(a, b[ch, pl.ds(3072, 1024), :], preferred_element_type=jnp.float32)


def far_own_kernel(b, q0, q1, p_own, tie, new):
    far_rows(b, q0, q1, 0, p_own, new)


def far_peer_kernel(pos, keep, flag, m, b, q0, q1, p_own, p_peer, new, out):
    lane = lax.broadcasted_iota(jnp.int32, (1, BLK), 1)
    eye = lax.broadcasted_iota(jnp.int32, (BLK, BLK), 0) == lax.broadcasted_iota(jnp.int32, (BLK, BLK), 1)
    chip, core = pos[1] * 4 + pos[2], pos[3]
    out[...] = jnp.zeros((1, BLK), jnp.float32)
    far_rows(b, q0, q1, 1, p_peer, new)

    def trace(block):
        line = jnp.sum(jnp.where(eye, block, 0.0), axis=0, keepdims=True)
        return jnp.sum(line, axis=1, keepdims=True)

    @pl.when(chip // 2 == pos[0])
    def _():
        total = jnp.zeros((1, BLK), jnp.float32)
        for ch in range(2):
            side = core if ch == 0 else 1 - core
            for j in range(2):
                i = (chip % 2) * 4 + side * 2 + j
                start = pl.multiple_of(i * BLK, BLK)
                rows, cols = pl.ds(start, BLK), pl.ds(j * BLK, BLK)
                if ch == 1:
                    block = new[rows, cols]
                else:
                    block = p_own[rows, cols]
                    for k in range(4):
                        a = (q0, q1)[k // 2][pl.ds(pl.multiple_of((k % 2) * 1024 + start, BLK), BLK), :]
                        block += jnp.dot(a, b[ch, pl.ds(3072 + k * 256, 256), cols], preferred_element_type=jnp.float32)
                total += jnp.where(lane == i, trace(block), 0.0)
                if ch == 0:
                    total += jnp.where(lane == 8 + i, keep[j, i].astype(jnp.float32), 0.0)
                    total += jnp.where(lane == 16 + i, trace(m[rows, cols].astype(jnp.float32)), 0.0)
                    total += jnp.where(lane == 24 + i, flag[i].astype(jnp.float32), 0.0)
        out[...] = total


def final_kernel(keep, flag, own, recv, m, out):
    for i in range(8):
        take = flag[i] == 1
        sign, twice = jnp.where(take, 1.0, -1.0), jnp.where(take, 0.0, 2.0)
        for j in range(2):
            at = (pl.ds(i * BLK, BLK), pl.ds(j * BLK, BLK))
            square = own[at] + recv[at]
            out[at] = (twice * m[at].astype(jnp.float32) + sign * square) * keep[j, i].astype(jnp.float32)


def bf16(*shape):
    return jax.ShapeDtypeStruct(shape, jnp.bfloat16)


def f32(*shape):
    return jax.ShapeDtypeStruct(shape, jnp.float32)


def trace_of(parts):
    spread = jnp.broadcast_to(parts[None], (128, 1, BLK))
    rows = lax.all_to_all(spread, ("row", Y, X), 0, 0).reshape(8, 16, BLK).sum(axis=1)
    rows = rows + lax.ppermute(rows, "layer", [(0, 1), (1, 0)])
    square, keep, linear, branch = (rows[:, 8 * n : 8 * n + 8] for n in range(4))
    return jnp.sum(keep * jnp.where(branch == 1.0, square, 2.0 * linear - square))


def on_device(density, block_mask, keep_mask, branch_flag):
    pos = jnp.stack([lax.axis_index(a) for a in ("row", Y, X, "layer")]).astype(jnp.int32)
    swap = [(0, 1), (1, 0)]
    m, own_rows, peer_rows = pl.pallas_call(
        mask_kernel,
        out_shape=[bf16(1024, 256), bf16(2, 256, 256), bf16(2, 256, 256)],
        in_specs=[SMEM, SMEM, VMEM],
        out_specs=[VMEM] * 3,
        compiler_params=room(6),
        name="mask",
    )(pos, block_mask.T, density)
    other = lax.ppermute(peer_rows, "layer", swap)
    z_tile = jnp.concatenate([own_rows, other], axis=0)
    z_plus, z_minus = ring8(z_tile, "row")
    line = jnp.concatenate([m, *(turn(m, 0, off) for off in (1, -1, 2))], axis=0)
    line_p, line_m, q0, q1 = ring4(line, 1)
    z_plus[2], _ = lax.optimization_barrier((z_plus[2], line_p))
    z_minus[2], _ = lax.optimization_barrier((z_minus[2], line_m))
    z_far = ring8_end(z_plus[2], z_minus[2], "row")
    inner = pl.pallas_call(
        rows_kernel,
        out_shape=bf16(2, 4096, 256),
        in_specs=[SMEM] + [VMEM] * 9,
        out_specs=VMEM,
        compiler_params=room(10),
        name="rows",
        cost_estimate=pl.CostEstimate(flops=int(HR * 1e9), bytes_accessed=8_000_000, transcendentals=0),
    )(pos, z_tile, *z_plus, *z_minus, *z_far)
    p_own, p_peer = pl.pallas_call(
        near_kernel,
        out_shape=[f32(1024, 256), f32(1024, 256)],
        in_specs=[VMEM] * 4,
        out_specs=[VMEM, VMEM],
        compiler_params=room(14),
        name="near",
        cost_estimate=pl.CostEstimate(flops=3_200_000_000, bytes_accessed=12_000_000, transcendentals=0),
    )(inner, line, line_p, line_m)
    keep = keep_mask.T
    peer_part, parts = pl.pallas_call(
        far_peer_kernel,
        out_shape=[f32(1024, 256), f32(1, BLK)],
        in_specs=[SMEM, SMEM, SMEM] + [VMEM] * 6,
        out_specs=[VMEM, VMEM],
        compiler_params=room(14),
        name="far_peer",
        cost_estimate=pl.CostEstimate(flops=540_000_000, bytes_accessed=4_000_000, transcendentals=0),
    )(pos, keep, branch_flag, m, inner, q0, q1, p_own, p_peer)
    own_part = pl.pallas_call(
        far_own_kernel,
        out_shape=f32(1024, 256),
        in_specs=[VMEM] * 5,
        out_specs=VMEM,
        compiler_params=room(10),
        name="far_own",
        cost_estimate=pl.CostEstimate(flops=540_000_000, bytes_accessed=4_000_000, transcendentals=0),
    )(inner, q0, q1, p_own, parts)
    recv = lax.ppermute(peer_part, "layer", swap)
    updated = pl.pallas_call(
        final_kernel,
        out_shape=f32(1024, 256),
        in_specs=[SMEM, SMEM, VMEM, VMEM, VMEM],
        out_specs=VMEM,
        compiler_params=room(6),
        name="final",
        cost_estimate=pl.CostEstimate(flops=2_000_000, bytes_accessed=4_000_000, transcendentals=0),
    )(keep, branch_flag, own_part, recv, m)
    return (updated, trace_of(parts))


def solution(mesh):
    split = Mesh(
        mesh.devices.reshape(mesh.shape["row"], 4, 4, mesh.shape["layer"]),
        ("row", Y, X, "layer"),
    )
    in_specs = (P("row", COL_LAYER), P("row", COL_LAYER), P("row", COL_LAYER), P("row"))
    out_specs = (P("row", COL_LAYER), P())
    return jax.shard_map(
        on_device, mesh=split, in_specs=in_specs, out_specs=out_specs, check_vma=False
    )
```

```python
import functools

import jax
import jax.numpy as jnp
from jax import lax
from jax.experimental import pallas as pl
from jax.experimental.pallas import tpu as pltpu
from jax.sharding import Mesh
from jax.sharding import PartitionSpec as P

BLK = 128
HZ = (6.0, 6.0, 2.0)
HR = 2.0
Y, X = "col_0", "col_1"
COL_LAYER = (Y, X, "layer")
SMEM = pl.BlockSpec(memory_space=pltpu.SMEM)
VMEM = pl.BlockSpec(memory_space=pltpu.VMEM)
HBM = pl.BlockSpec(memory_space=pl.ANY)


def room(mib):
    return pltpu.CompilerParams(vmem_limit_bytes=mib * 1024 * 1024)


def shift(value, axis, off):
    n = lax.axis_size(axis)
    return lax.ppermute(value, axis, [(i, (i + off) % n) for i in range(n)])


def turn(value, stage, off):
    nz, ny, nx = (lax.axis_size(a) for a in ("row", Y, X))
    at = lambda z, y, x, core: ((z * ny + y) * nx + x) * 2 + core
    pairs = []
    for z in range(nz):
        for y in range(ny):
            for x in range(nx):
                for core in range(2):
                    along_x = core == stage
                    to = (y, (x + off) % nx) if along_x else ((y + off) % ny, x)
                    pairs.append((at(z, y, x, core), at(z, *to, core)))
    return lax.ppermute(value, ("row", Y, X, "layer"), pairs)


def keep_kernel(x, out):
    pass


def hold(value, us):
    return pl.pallas_call(
        keep_kernel,
        out_shape=jax.ShapeDtypeStruct(value.shape, value.dtype),
        in_specs=[HBM],
        out_specs=HBM,
        input_output_aliases={0: 0},
        compiler_params=room(1),
        name="hold",
        cost_estimate=pl.CostEstimate(flops=int(us * 1e9), bytes_accessed=0, transcendentals=0),
    )(value)


def ring4(own, stage):
    half = own.shape[0] // 2
    plus, minus = turn(own, stage, 1), turn(own, stage, -1)
    return plus, minus, turn(plus[:half], stage, 1), turn(minus[half:], stage, -1)


def ring8(own, axis):
    plus, minus = [own], [own]
    for cost in HZ:
        plus.append(hold(shift(plus[-1], axis, 1), cost))
        minus.append(hold(shift(minus[-1], axis, -1), cost))
    return plus[1:], minus[1:]


def ring8_end(plus, minus, axis):
    half = plus.shape[0] // 2
    return shift(plus[:half], axis, 1), shift(minus[half:], axis, -1)


def mask_kernel(pos, bm, x, m, own, peer):
    layer = pos[3]
    rows = []
    for i in range(8):
        parts = [
            x[pl.ds(i * BLK, BLK), pl.ds(j * BLK, BLK)] * bm[j, i].astype(jnp.float32).astype(jnp.bfloat16)
            for j in range(2)
        ]
        rows.append(jnp.concatenate(parts, axis=1))
    for i in range(8):
        m[pl.ds(i * BLK, BLK), :] = rows[i]
        at, cls, inner = i // 4, (i // 2) % 2, i % 2

        @pl.when(layer == cls)
        def _():
            own[at, pl.ds(inner * BLK, BLK), :] = rows[i]

        @pl.when(layer != cls)
        def _():
            peer[at, pl.ds(inner * BLK, BLK), :] = rows[i]


def place(pos, d, half):
    r, y, x = pos[0], pos[1], pos[2]
    src = lax.rem(r - d + 8, 8)
    col = src * 2 + half
    dy, dx = lax.rem(col // 4 - y + 4, 4), lax.rem(lax.rem(col, 4) - x + 4, 4)
    rank = lambda o: jnp.where(o == 0, 0, jnp.where(o == 3, 1, jnp.where(o == 1, 2, 3)))
    return rank(dy), rank(dx)


def rows_kernel(pos, *refs):
    z_refs, b = refs[:9], refs[9]
    pieces = [(d, ch, rh, d, 2 * ch + rh) for d in range(4) for ch in range(2) for rh in range(2)]
    pieces += [(-d, ch, rh, 3 + d, 2 * ch + rh) for d in range(1, 4) for ch in range(2) for rh in range(2)]
    pieces += [(4, ch, rh, 7 + ch, rh) for ch in range(2) for rh in range(2)]
    for d, ch, rh, ref, at in pieces:
        ry, rx = place(pos, d, rh)
        to = jnp.where(pos[3] == 0, ry * 4 + rx, rx * 4 + ry)
        b[ch, pl.ds(pl.multiple_of(to * 256, 256), 256), :] = z_refs[ref][at]


def near_kernel(b, line, line_p, line_m, p_own, p_peer):
    @pl.loop(0, 4)
    def _(i):
        a = []
        for src in (line, line_p, line_m):
            for k in range(4):
                a.append(src[pl.ds(pl.multiple_of(k * 1024 + i * 256, 256), 256), :])
        rows = pl.ds(pl.multiple_of(i * 256, 256), 256)
        a = jnp.concatenate(a, axis=1)
        p_peer[rows, :] = jnp.dot(a, b[1, pl.ds(0, 3072), :], preferred_element_type=jnp.float32)
        p_own[rows, :] = jnp.dot(a, b[0, pl.ds(0, 3072), :], preferred_element_type=jnp.float32)


def far_rows(b, q0, q1, ch, old, new):
    for i in range(4):
        rows = pl.ds(i * 256, 256)
        a = jnp.concatenate([(q0, q1)[k // 2][pl.ds((k % 2) * 1024 + i * 256, 256), :] for k in range(4)], axis=1)
        new[rows, :] = old[rows, :] + jnp.dot(a, b[ch, pl.ds(3072, 1024), :], preferred_element_type=jnp.float32)


def far_peer_kernel(pos, keep, flag, m, b, q0, q1, p_own, p_peer, new, out):
    lane = lax.broadcasted_iota(jnp.int32, (1, BLK), 1)
    eye = lax.broadcasted_iota(jnp.int32, (BLK, BLK), 0) == lax.broadcasted_iota(jnp.int32, (BLK, BLK), 1)
    chip, core = pos[1] * 4 + pos[2], pos[3]
    out[...] = jnp.zeros((1, BLK), jnp.float32)
    far_rows(b, q0, q1, 1, p_peer, new)

    def trace(block):
        line = jnp.sum(jnp.where(eye, block, 0.0), axis=0, keepdims=True)
        return jnp.sum(line, axis=1, keepdims=True)

    @pl.when(chip // 2 == pos[0])
    def _():
        total = jnp.zeros((1, BLK), jnp.float32)
        for ch in range(2):
            side = core if ch == 0 else 1 - core
            for j in range(2):
                i = (chip % 2) * 4 + side * 2 + j
                start = pl.multiple_of(i * BLK, BLK)
                rows, cols = pl.ds(start, BLK), pl.ds(j * BLK, BLK)
                if ch == 1:
                    block = new[rows, cols]
                else:
                    block = p_own[rows, cols]
                    for k in range(4):
                        a = (q0, q1)[k // 2][pl.ds(pl.multiple_of((k % 2) * 1024 + start, BLK), BLK), :]
                        block += jnp.dot(a, b[ch, pl.ds(3072 + k * 256, 256), cols], preferred_element_type=jnp.float32)
                total += jnp.where(lane == i, trace(block), 0.0)
                if ch == 0:
                    total += jnp.where(lane == 8 + i, keep[j, i].astype(jnp.float32), 0.0)
                    total += jnp.where(lane == 16 + i, trace(m[rows, cols].astype(jnp.float32)), 0.0)
                    total += jnp.where(lane == 24 + i, flag[i].astype(jnp.float32), 0.0)
        out[...] = total


def final_kernel(keep, flag, b, q0, q1, p_own, recv, m, out):
    for n in range(4):
        rows = pl.ds(n * 256, 256)
        a = jnp.concatenate([(q0, q1)[k // 2][pl.ds((k % 2) * 1024 + n * 256, 256), :] for k in range(4)], axis=1)
        product = jnp.dot(a, b[0, pl.ds(3072, 1024), :], preferred_element_type=jnp.float32)
        square = p_own[rows, :] + recv[rows, :] + product
        for i in (2 * n, 2 * n + 1):
            take = flag[i] == 1
            sign, twice = jnp.where(take, 1.0, -1.0), jnp.where(take, 0.0, 2.0)
            for j in range(2):
                at = (pl.ds(i * BLK, BLK), pl.ds(j * BLK, BLK))
                part = square[(i % 2) * BLK : (i % 2 + 1) * BLK, j * BLK : (j + 1) * BLK]
                out[at] = (twice * m[at].astype(jnp.float32) + sign * part) * keep[j, i].astype(jnp.float32)


def bf16(*shape):
    return jax.ShapeDtypeStruct(shape, jnp.bfloat16)


def f32(*shape):
    return jax.ShapeDtypeStruct(shape, jnp.float32)


def over_planes(parts):
    spread = jnp.broadcast_to(parts[None], (64, 1, BLK))
    planes = lax.all_to_all(spread, ("row", Y, "layer"), 0, 0).reshape(8, 8, BLK).sum(axis=1)
    return [planes] + [lax.ppermute(planes, X, [(i, i ^ bits) for i in range(4)]) for bits in (1, 3, 2)]


def trace_of(values):
    rows = functools.reduce(jnp.add, values)
    square, keep, linear, branch = (rows[:, 8 * n : 8 * n + 8] for n in range(4))
    return jnp.sum(keep * jnp.where(branch == 1.0, square, 2.0 * linear - square))


def on_device(density, block_mask, keep_mask, branch_flag):
    pos = jnp.stack([lax.axis_index(a) for a in ("row", Y, X, "layer")]).astype(jnp.int32)
    swap = [(0, 1), (1, 0)]
    m, own_rows, peer_rows = pl.pallas_call(
        mask_kernel,
        out_shape=[bf16(1024, 256), bf16(2, 256, 256), bf16(2, 256, 256)],
        in_specs=[SMEM, SMEM, VMEM],
        out_specs=[VMEM] * 3,
        compiler_params=room(6),
        name="mask",
    )(pos, block_mask.T, density)
    other = lax.ppermute(peer_rows, "layer", swap)
    z_tile = jnp.concatenate([own_rows, other], axis=0)
    z_plus, z_minus = ring8(z_tile, "row")
    line = jnp.concatenate([m, *(turn(m, 0, off) for off in (1, -1, 2))], axis=0)
    line_p, line_m, q0, q1 = ring4(line, 1)
    z_plus[2], _ = lax.optimization_barrier((z_plus[2], line_p))
    z_minus[2], _ = lax.optimization_barrier((z_minus[2], line_m))
    z_far = ring8_end(z_plus[2], z_minus[2], "row")
    inner = pl.pallas_call(
        rows_kernel,
        out_shape=bf16(2, 4096, 256),
        in_specs=[SMEM] + [VMEM] * 9,
        out_specs=VMEM,
        compiler_params=room(10),
        name="rows",
        cost_estimate=pl.CostEstimate(flops=int(HR * 1e9), bytes_accessed=8_000_000, transcendentals=0),
    )(pos, z_tile, *z_plus, *z_minus, *z_far)
    p_own, p_peer = pl.pallas_call(
        near_kernel,
        out_shape=[f32(1024, 256), f32(1024, 256)],
        in_specs=[VMEM] * 4,
        out_specs=[VMEM, VMEM],
        compiler_params=room(14),
        name="near",
        cost_estimate=pl.CostEstimate(flops=3_200_000_000, bytes_accessed=12_000_000, transcendentals=0),
    )(inner, line, line_p, line_m)
    keep = keep_mask.T
    peer_part, parts = pl.pallas_call(
        far_peer_kernel,
        out_shape=[f32(1024, 256), f32(1, BLK)],
        in_specs=[SMEM, SMEM, SMEM] + [VMEM] * 6,
        out_specs=[VMEM, VMEM],
        compiler_params=room(14),
        name="far_peer",
        cost_estimate=pl.CostEstimate(flops=540_000_000, bytes_accessed=4_000_000, transcendentals=0),
    )(pos, keep, branch_flag, m, inner, q0, q1, p_own, p_peer)
    recv = lax.ppermute(peer_part, "layer", swap)
    updated = pl.pallas_call(
        final_kernel,
        out_shape=f32(1024, 256),
        in_specs=[SMEM, SMEM] + [VMEM] * 6,
        out_specs=VMEM,
        compiler_params=room(12),
        name="final",
        cost_estimate=pl.CostEstimate(flops=2_000_000, bytes_accessed=4_000_000, transcendentals=0),
    )(keep, branch_flag, inner, q0, q1, p_own, recv, m)
    updated, values = lax.optimization_barrier((updated, over_planes(parts)))
    return (updated, trace_of(values))


def solution(mesh):
    split = Mesh(
        mesh.devices.reshape(mesh.shape["row"], 4, 4, mesh.shape["layer"]),
        ("row", Y, X, "layer"),
    )
    in_specs = (P("row", COL_LAYER), P("row", COL_LAYER), P("row", COL_LAYER), P("row"))
    out_specs = (P("row", COL_LAYER), P())
    return jax.shard_map(
        on_device, mesh=split, in_specs=in_specs, out_specs=out_specs, check_vma=False
    )
```
